1024 devices in a mesh: row: 128 (over z, x, core), col: 8 (over y).
Axes of the slice: x: 8, y: 8, z: 8, core: 2. Of those that a mesh axis runs over, the one named last changes fastest.
Arguments:
- velocity: float32 [8, 128, 7, 3, 4096], P('col', 'row'), may hold values from -6 to 6
- counts: int32 [8, 128], P('col', 'row'), may hold values from 1 to 7, as said below
Outputs:
- compressive: float32 [8, 128, 7, 3, 4096], P('col', 'row')
- solenoidal: float32 [8, 128, 7, 3, 4096], P('col', 'row')
The draws below stay inside these ranges and needn't reach their ends.
Inputs may be any that keep to these rules, and one draw needn't show every extreme that they name: In every column c, owners 2t and 2t+1 hold 8 blocks together: counts[c, 2t] + counts[c, 2t+1] = 8. 7 is reached in every column.
All inputs are finite; a program needn't handle non-finite values.
Results may differ from the reference program's by a relative error of at most 0.000096.
Values sent between devices are 32-bit elements; how exact they have to be, the bound alone decides.
A program may use at most 64 MiB of HBM per device.

```python
import jax
import jax.numpy as jnp

BLK = 16
SLOTS = 7
XB = 4
XBR = 16
ZBR = 8
NX = 256
NY = 256
NZ = 256
N_ROW = 128
N_COL = 8


def draw_counts(key, part):
    pairs = N_ROW // 2
    key_extra, key_chosen, key_flip = jax.random.split(key, 3)
    extra = jax.random.randint(key_extra, (N_COL, pairs), -3, 4)
    chosen = jax.random.randint(key_chosen, (N_COL, 1), 0, pairs)
    flipped = jax.random.randint(key_flip, (N_COL, 1), 0, 2)
    placed = jnp.arange(pairs, dtype=jnp.int32)[None, :]
    extra = jnp.where(placed == chosen, 3 - 6 * flipped, extra)
    return jnp.stack([4 + extra, 4 - extra], axis=-1).reshape(N_COL, N_ROW).astype(jnp.int32)


def levels(own_key, shape, cuts, smallest, largest):
    loudness, own = 1.0, jax.random.fold_in(own_key, 6)
    for axis_at, shards_of in cuts:
        heights = jnp.exp(jax.random.uniform(jax.random.fold_in(own, axis_at), (shards_of,), jnp.float32, smallest / len(cuts), largest / len(cuts)))
        loudness = loudness * jnp.repeat(heights, shape[axis_at] // shards_of).reshape([-1 if axis == axis_at else 1 for axis in range(len(shape))])
    return loudness


def centred(rng, dims, width, reach, pieces=(), kind=jnp.bfloat16):
    gain = levels(rng, dims, pieces, -0.22, 0.18) if pieces else 1.0
    array = jax.random.normal(rng, dims, jnp.float32) * width * gain
    return jnp.minimum(jnp.maximum(array, -reach), reach).astype(kind)


def setup_inputs(seed: int = 0) -> dict:
    key_list = jax.random.split(jax.random.key(seed), 3)
    velocity = centred(key_list[0], (N_COL, N_ROW, SLOTS, 3, BLK**3), 1.0, 6.0, ((0, 8), (1, 128)), jnp.float32)
    counts = draw_counts(jax.random.fold_in(key_list[2], 71), 0)
    return {"velocity": velocity, "counts": counts}


def collect_bits(number, first_bit, bit_count):
    summed = number * 0
    for bit_step in range(bit_count):
        summed = summed + ((number >> (first_bit + 2 * bit_step)) & 1) * (1 << bit_step)
    return summed


def signed_wave(length):
    indices = jnp.arange(length, dtype=jnp.int32)
    waves = jnp.where(indices > length // 2, indices - length, indices)
    waves = jnp.where(indices == length // 2, 0, waves)
    return waves.astype(jnp.float32)


def reference(velocity, counts):
    owners = jnp.arange(N_ROW, dtype=jnp.int32)[None, :]
    starts = 4 * owners + (owners % 2) * (4 - counts)
    column = jnp.arange(N_COL, dtype=jnp.int32)[:, None, None]
    bricks = jnp.arange(N_ROW, dtype=jnp.int32)[None, :, None]
    quarter = jnp.arange(4, dtype=jnp.int32)[None, None, :]
    block_keys = 4 * bricks + quarter
    pair_first = 2 * (bricks // 2)
    first_count = counts[column, pair_first]
    owner_of = jnp.where(block_keys - 4 * pair_first < first_count, pair_first, pair_first + 1)
    slot_of = block_keys - starts[column, owner_of]
    gathered = velocity[column, owner_of, slot_of]
    grid_cells = gathered.reshape(N_COL, N_ROW, 2, 2, 3, BLK, BLK, BLK)
    grid_cells = grid_cells.transpose(0, 1, 4, 5, 3, 6, 2, 7).reshape(N_COL, N_ROW, 3, BLK, 2 * BLK, 2 * BLK)
    brick_ids = jnp.arange(N_ROW, dtype=jnp.int32)
    placed = collect_bits(brick_ids, 0, XB) * ZBR + collect_bits(brick_ids, 1, XB - 1)
    ordered = jnp.zeros_like(grid_cells).at[:, placed].set(grid_cells)
    ordered = ordered.reshape(N_COL, XBR, ZBR, 3, BLK, 2 * BLK, 2 * BLK)
    velocity_field = ordered.transpose(3, 1, 4, 0, 5, 2, 6).reshape(3, NX, NY, NZ)
    wave_x = signed_wave(NX)[:, None, None]
    wave_y = signed_wave(NY)[None, :, None]
    wave_z = signed_wave(NZ)[None, None, :]
    waves = (wave_x, wave_y, wave_z)
    numerator = wave_x * jnp.fft.fftn(velocity_field[0])
    numerator = numerator + wave_y * jnp.fft.fftn(velocity_field[1])
    numerator = numerator + wave_z * jnp.fft.fftn(velocity_field[2])
    square_sum = jnp.maximum(wave_x * wave_x + wave_y * wave_y + wave_z * wave_z, 1.0)
    potential = numerator / square_sum
    parts = [jnp.real(jnp.fft.ifftn(waves[comp_id] * potential)) for comp_id in range(3)]
    compressive_field = jnp.stack(parts).astype(jnp.float32)
    back = compressive_field.reshape(3, XBR, BLK, N_COL, 2 * BLK, ZBR, 2 * BLK)
    back = back.transpose(3, 1, 5, 0, 2, 4, 6).reshape(N_COL, XBR * ZBR, 3, BLK, 2 * BLK, 2 * BLK)
    back = back[:, placed]
    back = back.reshape(N_COL, N_ROW, 3, BLK, 2, BLK, 2, BLK)
    comp_blocks = back.transpose(0, 1, 6, 4, 2, 3, 5, 7).reshape(N_COL, N_ROW, 4, 3, BLK ** 3)
    slot_ids = jnp.arange(SLOTS, dtype=jnp.int32)[None, None, :]
    slot_keys = starts[:, :, None] + slot_ids
    in_use = (slot_ids < counts[:, :, None])[:, :, :, None, None]
    home_brick = jnp.clip(slot_keys // 4, 0, N_ROW - 1)
    picked = comp_blocks[column, home_brick, slot_keys % 4]
    compressive = jnp.where(in_use, picked, 0.0)
    solenoidal = jnp.where(in_use, velocity - compressive, 0.0)
    return compressive, solenoidal
```

```python
import jax
import jax.numpy as jnp
import ml_dtypes
import numpy as np
from jax import lax
from jax.experimental import pallas as pl
from jax.experimental.pallas import tpu as pltpu
from jax.sharding import PartitionSpec as P

MESH = pl.DeviceIdType.MESH
SLOTS = 7
N = 256
F32 = jnp.float32
BF16 = jnp.bfloat16


def split_np(table):
    head = table.astype(ml_dtypes.bfloat16)
    rest = (table - head.astype(np.float64)).astype(ml_dtypes.bfloat16)
    return head, rest


def weights():
    at = np.arange(N)
    angle = 2 * np.pi * ((at[:, None] * at[None, :]) % N) / N
    cos, sin = np.cos(angle), np.sin(angle)
    e_lo, e_hi, py, j0 = np.meshgrid(np.arange(8), np.arange(2), np.arange(8), np.arange(2), indexing="ij")
    y_of = (32 * py + 16 * j0 + 8 * e_hi + e_lo).reshape(-1)
    real_rows, imag_rows = cos[:128], -sin[:128].copy()
    imag_rows[0] = cos[128]
    forward = np.stack([real_rows.reshape(16, 8, N), imag_rows.reshape(16, 8, N)], axis=1).reshape(N, N)
    gain = np.full((128, 1), 2.0)
    gain[0] = 1.0
    back = np.stack([(gain * real_rows).reshape(16, 8, N), (gain * imag_rows).reshape(16, 8, N)], axis=1).reshape(N, N)
    back = back.T / float(N) ** 3
    both = np.concatenate([cos, sin], axis=1)
    return (*split_np(both), *split_np(forward[:, y_of]), *split_np(back[y_of]))


def lane_roll(value, shift):
    return pltpu.roll(value, shift % 128, value.ndim - 1)


def lane_bit(shape, bit):
    return (lax.broadcasted_iota(jnp.int32, shape, len(shape) - 1) // (1 << bit)) % 2 == 1


def swap_bit(low, high, bit):
    upper = lane_bit(low.shape, bit)
    step = 1 << bit
    return jnp.where(upper, lane_roll(high, step), low), jnp.where(upper, high, lane_roll(low, -step))


def swap_bits(items, pairs):
    items = list(items)
    for index_bit, bit in pairs:
        for at in range(len(items)):
            if not (at >> index_bit) & 1:
                other = at | (1 << index_bit)
                items[at], items[other] = swap_bit(items[at], items[other], bit)
    return items


def halves(value):
    head = value.astype(BF16)
    return head, (value - head.astype(F32)).astype(BF16)


def dot(left, right):
    return lax.dot_general(left, right, (((1,), (0,)), ((), ())), preferred_element_type=F32)


def dot_left(head, rest, value):
    value_head, value_rest = halves(value)
    return dot(head, value_head) + (dot(head, value_rest) + dot(rest, value_head))


def dot_right(value, head, rest):
    value_head, value_rest = halves(value)
    return dot(value_head, head) + (dot(value_rest, head) + dot(value_head, rest))


def signed(index):
    return jnp.where(index == N // 2, 0, jnp.where(index > N // 2, index - N, index)).astype(F32)


def spread(number):
    return (number & 1) + 2 * (number & 2) + 4 * (number & 4) + 8 * (number & 8)


def gathered_bits(number):
    return (number & 1) + ((number >> 1) & 2) + ((number >> 2) & 4) + ((number >> 3) & 8)


def stage_y(r1, s2, wy_h, wy_l):
    def lines(d):
        return [
            jnp.concatenate([r1[d, pl.ds(2 * a + e, 16, stride=8), :] for e in range(2)], axis=0) for a in range(4)
        ]

    pair = swap_bits(lines(0) + lines(1), [(0, 4), (1, 5), (2, 6)])
    lone = swap_bits(lines(2), [(0, 4), (1, 5)])
    turned = [lane_roll(item, 64) for item in lone]
    upper = lane_bit((32, 128), 6)
    lone = [jnp.where(upper, b, a) for a, b in zip(lone, turned)] + [jnp.where(upper, a, b) for a, b in zip(lone, turned)]
    both = jnp.concatenate([jnp.concatenate(pair, axis=0), jnp.concatenate(lone, axis=0)], axis=1)
    out = dot_left(wy_h[...], wy_l[...], both)
    s2[:, 0:16, :] = out[:, :128].reshape(16, 16, 128)
    last = out[:, 128:].reshape(16, 2, 8, 128)
    s2[:, 16:24, :] = jnp.where(lane_bit((16, 8, 128), 6), last[:, 1], last[:, 0])


def stage_z(r2, s3, cs_h, cs_l, wave_y):
    tiles = []
    for high in range(2):
        items = [r2[8 * high + low] for low in range(8)]
        tiles.append(swap_bits(items, [(0, 4), (1, 5), (2, 6)]))
    left = jnp.concatenate([jnp.concatenate([tiles[0][i], tiles[1][i]], axis=1) for i in range(8)], axis=0)
    out = dot_right(left, cs_h[...], cs_l[...]).reshape(8, 3, 8, 512)
    by_cos, by_sin = out[..., :256], out[..., 256:]
    kz = lax.broadcasted_iota(jnp.int32, (8, 256), 1)
    wave_z = signed(kz)
    wy = wave_y(lax.broadcasted_iota(jnp.int32, (8, 256), 0))
    for a in range(4):
        first = (by_cos[a, 0] + by_sin[a, 1], by_cos[a, 1] - by_sin[a, 0])
        b = 4 + a
        second = (by_cos[b, 0] + by_sin[b, 1], by_cos[b, 1] - by_sin[b, 0])
        third = (by_cos[a, 2] + by_sin[b, 2], by_cos[b, 2] - by_sin[a, 2])
        rest = tuple(wy * second[i] + wave_z * third[i] for i in range(2))
        for h in range(2):
            lanes = slice(128 * h, 128 * h + 128)
            items = [first[0][:, lanes], first[1][:, lanes], rest[0][:, lanes], rest[1][:, lanes]]
            items = swap_bits(items, [(0, 5), (1, 6)])
            for q in range(4):
                s3[pl.ds((4 * h + q) * 32 + a, 8, stride=4), :] = items[q]


def stage_x(r3, s4, cs_h, cs_l, ky, kz_high):
    shape = (N, 128)
    lane = lax.broadcasted_iota(jnp.int32, shape, 1)
    kx = lax.broadcasted_iota(jnp.int32, shape, 0)
    imag = lane_bit(shape, 5)
    value = r3[...]
    turned = jnp.where(imag, -lane_roll(value, 32), lane_roll(value, -32))
    out = dot_left(cs_h[...], cs_l[...], jnp.concatenate([value, turned], axis=0))
    wave_x = signed(kx)
    wave_z = signed(32 * kz_high + lane % 32)
    wave_y = ky.astype(F32)
    square_sum = jnp.maximum(wave_x * wave_x + wave_y * wave_y + wave_z * wave_z, 1.0)
    factor = jnp.where(lane_bit(shape, 6), 1.0, wave_x)
    terms = factor * out
    fields = (terms + lane_roll(terms, 64)) / square_sum * factor
    turned = jnp.where(imag, lane_roll(fields, 32), -lane_roll(fields, -32))
    s4[...] = dot_left(cs_h[...], cs_l[...], jnp.concatenate([fields, turned], axis=0))


def stage_z_back(r4, s5, cs_h, cs_l, wave_y):
    wave_z = signed(lax.broadcasted_iota(jnp.int32, (8, 256), 1))
    wy = wave_y(lax.broadcasted_iota(jnp.int32, (8, 256), 0))
    rows = [None] * 8
    for a in range(4):
        sides = []
        for h in range(2):
            items = [r4[pl.ds((4 * h + q) * 32 + a, 8, stride=4), :] for q in range(4)]
            sides.append(swap_bits(items, [(0, 5), (1, 6)]))
        first = [jnp.concatenate([sides[0][i], sides[1][i]], axis=1) for i in range(2)]
        pot = [jnp.concatenate([sides[0][2 + i], sides[1][2 + i]], axis=1) for i in range(2)]
        rows[a] = jnp.concatenate([first[0], first[1], wave_z * pot[0]], axis=0)
        rows[4 + a] = jnp.concatenate([wy * pot[0], wy * pot[1], wave_z * pot[1]], axis=0)
    out = dot_right(jnp.concatenate(rows, axis=0), cs_h[...], cs_l[...]).reshape(8, 3, 8, 512)
    by_cos, by_sin = out[..., :256], out[..., 256:]
    items = [None] * 8
    for a in range(4):
        b = 4 + a
        items[a] = jnp.concatenate(
            [by_cos[a, 0] - by_sin[a, 1], by_cos[a, 1] + by_sin[a, 0], by_cos[a, 2] - by_sin[b, 2]], axis=0
        )
        items[b] = jnp.concatenate(
            [by_cos[b, 0] - by_sin[b, 1], by_cos[b, 1] + by_sin[b, 0], by_cos[b, 2] + by_sin[a, 2]], axis=0
        )
    for high in range(2):
        tile = swap_bits([item[:, 128 * high : 128 * high + 128] for item in items], [(0, 4), (1, 5), (2, 6)])
        for low in range(8):
            s5[8 * high + low] = tile[low]


def stage_y_back(r5, s6, vy_h, vy_l):
    pair = r5[:, 0:16, :].reshape(N, 128)
    last = r5[:, 16:24, :]
    last = jnp.stack([last, lane_roll(last, 64)], axis=1).reshape(N, 128)
    out = dot_left(vy_h[...], vy_l[...], jnp.concatenate([pair, last], axis=1))
    pair = swap_bits([out[32 * i : 32 * i + 32, :128] for i in range(8)], [(0, 4), (1, 5), (2, 6)])
    last = [out[32 * i : 32 * i + 32, 128:] for i in range(8)]
    upper = lane_bit((32, 128), 6)
    last = swap_bits([jnp.where(upper, lane_roll(last[4 + i], 64), last[i]) for i in range(4)], [(0, 4), (1, 5)])
    for d, items in enumerate((pair[:4], pair[4:], last)):
        for a in range(4):
            for e in range(2):
                s6[d, pl.ds(2 * a + e, 16, stride=8), :] = items[a][16 * e : 16 * e + 16]


def kernel(
    vel, cnt, cs_h, cs_l, wy_h, wy_l, vy_h, vy_l, comp, sol,
    s0, r0, s1, r1, s2, r2, s3, r3, s4, r4, s5, r5, s6, r6, cb, r7, send, recv,
):
    row, col = lax.axis_index("row"), lax.axis_index("col")
    core = row & 1
    j1, a_hi = col & 1, col >> 1
    px, pz = gathered_bits(row), gathered_bits(row >> 1)
    xi = 4 * px + a_hi
    zi = 2 * pz + j1

    def peer_x(step):
        return (row ^ spread(step >> 2), col ^ (2 * (step & 3)))

    def peer_z(step):
        return (row ^ (2 * spread(step >> 1)), col ^ (step & 1))

    def peer_y(step):
        return (row, col ^ step)

    partner = (row ^ 1, col)

    barrier = pltpu.get_barrier_semaphore()
    for peer, count in ((peer_y, 8), (peer_z, 16), (peer_x, 64)):

        @pl.loop(1, count)
        def _(step, peer=peer):
            pl.semaphore_signal(barrier, inc=1, device_id=peer(step), device_id_type=MESH)

    pl.semaphore_wait(barrier, 7 + 15 + 63)

    def put(source, target, phase, device):
        pltpu.make_async_remote_copy(
            src_ref=source, dst_ref=target, send_sem=send.at[phase], recv_sem=recv.at[phase],
            device_id=device, device_id_type=MESH,
        ).start()

    def keep(source, target, phase):
        pltpu.make_async_copy(source, target, recv.at[phase]).start()

    def arrived(buffer, phase):
        pltpu.make_async_copy(buffer, buffer, recv.at[phase]).wait()

    def left(part, phase):
        pltpu.make_async_copy(part, part, send.at[phase]).wait()

    count = cnt[0, 0]
    for i in range(3):
        s0[i] = vel[jnp.where(core == 1, jnp.maximum(count - 7 + i, 0), 4 + i)]
    put(s0, r0, 0, partner)
    arrived(r0, 0)
    for j in range(4):
        slot = jnp.where(core == 1, count - 4 + j, j)
        owned = jnp.where(core == 1, slot >= 0, j < count)
        mine = vel[jnp.clip(slot, 0, SLOTS - 1)]
        theirs = r0[jnp.clip(jnp.where(core == 1, j, j - 1), 0, 2)]
        block = jnp.where(owned, mine, theirs)
        for d in range(3):
            for quad in range(4):
                at = (2 * quad + j // 2) * 16 + (j % 2) * 8
                s1[d, at : at + 8, :] = block[d, 8 * quad : 8 * quad + 8]

    def exchange_y(source, target, phase):
        for d in range(3):

            @pl.loop(1, 8)
            def _(step, d=d):
                there = pl.multiple_of(16 * (col ^ step), 16)
                here = pl.multiple_of(16 * col, 16)
                put(source.at[d, pl.ds(there, 16)], target.at[d, pl.ds(here, 16)], phase, peer_y(step))

        here = pl.multiple_of(16 * col, 16)
        keep(source.at[:, pl.ds(here, 16)], target.at[:, pl.ds(here, 16)], phase)
        arrived(target, phase)

    def exchange_z(source, target, phase):
        @pl.loop(1, 16)
        def _(step):
            put(source.at[zi ^ step], target.at[zi], phase, peer_z(step))

        keep(source.at[zi], target.at[zi], phase)
        arrived(target, phase)

    def exchange_x(source, target, phase):
        here = pl.multiple_of(4 * xi, 4)

        @pl.loop(1, 64)
        def _(step):
            there = pl.multiple_of(4 * (xi ^ step), 4)
            put(source.at[pl.ds(there, 4)], target.at[pl.ds(here, 4)], phase, peer_x(step))

        keep(source.at[pl.ds(here, 4)], target.at[pl.ds(here, 4)], phase)
        arrived(target, phase)

    def wave_y(k):
        return (8 * zi + k).astype(F32)

    exchange_y(s1, r1, 1)
    stage_y(r1, s2, wy_h, wy_l)
    exchange_z(s2, r2, 2)
    stage_z(r2, s3, cs_h, cs_l, wave_y)
    exchange_x(s3, r3, 3)
    stage_x(r3, s4, cs_h, cs_l, 8 * zi + (xi & 7), xi >> 3)
    exchange_x(s4, r4, 4)
    stage_z_back(r4, s5, cs_h, cs_l, wave_y)
    exchange_z(s5, r5, 5)
    stage_y_back(r5, s6, vy_h, vy_l)
    exchange_y(s6, r6, 6)
    for j in range(4):
        for d in range(3):
            for quad in range(4):
                at = (2 * quad + j // 2) * 16 + (j % 2) * 8
                cb[j, d, 8 * quad : 8 * quad + 8, :] = r6[d, at : at + 8, :]
    put(cb.at[pl.ds(1 - core, 3)], r7, 7, partner)
    arrived(r7, 7)
    for s in range(SLOTS):
        key = jnp.where(core == 1, 8 - count, 0) + s
        mine = cb[jnp.clip(key - 4 * core, 0, 3)]
        theirs = r7[jnp.clip(jnp.where(core == 1, key - 1, key - 4), 0, 2)]
        used = s < count
        value = jnp.where(used, jnp.where((key >> 2) == core, mine, theirs), 0.0)
        comp[s] = value
        sol[s] = jnp.where(used, vel[s] - value, 0.0)

    left(s0, 0)
    left(s1.at[:, pl.ds(0, 112)], 1)
    left(s2.at[pl.ds(0, 15)], 2)
    left(s3.at[pl.ds(0, 252)], 3)
    left(s4.at[pl.ds(0, 252)], 4)
    left(s5.at[pl.ds(0, 15)], 5)
    left(s6.at[:, pl.ds(0, 112)], 6)
    left(cb.at[pl.ds(0, 3)], 7)


def body(velocity, counts):
    vmem = pl.BlockSpec(memory_space=pltpu.VMEM)
    blocks = velocity.reshape(SLOTS, 3, 32, 128)
    shape = jax.ShapeDtypeStruct((SLOTS, 3, 32, 128), F32)
    tables = [jnp.asarray(table) for table in weights()]
    part = pltpu.VMEM((3, 3, 32, 128), F32)
    fields = pltpu.VMEM((3, 128, 128), F32)
    lines = pltpu.VMEM((16, 24, 128), F32)
    pencils = pltpu.VMEM((N, 128), F32)
    comp, sol = pl.pallas_call(
        kernel,
        out_shape=(shape, shape),
        in_specs=[vmem, pl.BlockSpec(memory_space=pltpu.SMEM)] + [vmem] * 6,
        out_specs=(vmem, vmem),
        scratch_shapes=[
            part, part, fields, fields, lines, lines, pencils, pencils, pencils, pencils, lines, lines, fields, fields,
            pltpu.VMEM((4, 3, 32, 128), F32), part,
            pltpu.SemaphoreType.DMA((8,)), pltpu.SemaphoreType.DMA((8,)),
        ],
        compiler_params=pltpu.CompilerParams(
            collective_id=0, has_side_effects=True, vmem_limit_bytes=32 * 1024 * 1024
        ),
        name="helmholtz",
    )(blocks, counts, *tables)
    return comp.reshape(velocity.shape), sol.reshape(velocity.shape)


def solution(mesh):
    blocks, owners = P("col", "row", None, None, None), P("col", "row")
    return jax.shard_map(body, mesh=mesh, in_specs=(blocks, owners), out_specs=(blocks, blocks), check_vma=False)
```

```python
import jax
import jax.numpy as jnp
import ml_dtypes
import numpy as np
from jax import lax
from jax.experimental import pallas as pl
from jax.experimental.pallas import tpu as pltpu
from jax.sharding import PartitionSpec as P

MESH = pl.DeviceIdType.MESH
SLOTS = 7
N = 256
F32 = jnp.float32
BF16 = jnp.bfloat16


def split_np(table):
    head = table.astype(ml_dtypes.bfloat16)
    rest = (table - head.astype(np.float64)).astype(ml_dtypes.bfloat16)
    return head, rest


def weights():
    at = np.arange(N)
    angle = 2 * np.pi * ((at[:, None] * at[None, :]) % N) / N
    cos, sin = np.cos(angle), np.sin(angle)
    high, brick, low = np.meshgrid(np.arange(4), np.arange(16), np.arange(4), indexing="ij")
    x_of = (16 * brick + 4 * high + low).reshape(-1)
    odd, pair = np.meshgrid(np.arange(2), np.arange(64), indexing="ij")
    k_of = (2 * pair + odd).reshape(-1)
    real_rows, imag_rows = cos[:128], -sin[:128].copy()
    imag_rows[0] = cos[128]
    gain = np.full((128, 1), 2.0)
    gain[0] = 1.0
    forward = np.concatenate([real_rows[k_of], imag_rows[k_of]], axis=0)
    back = np.concatenate([(gain * real_rows)[k_of], (gain * imag_rows)[k_of]], axis=0).T
    low, source = np.meshgrid(np.arange(4), np.arange(64), indexing="ij")
    z_of = (4 * source + low).reshape(-1)
    lane = np.arange(N)
    bit = lambda b: (lane >> b) & 1
    y_of = 128 * bit(7) + 64 * bit(3) + 32 * bit(1) + 16 * bit(0) + 8 * bit(2) + ((lane >> 4) & 7)
    both = lambda rows, columns: np.concatenate([t[rows][:, columns] for t in (cos, sin)], axis=1)
    x_both = np.concatenate([forward[:, x_of], back[x_of]], axis=1)
    tables = x_both, both(at, z_of), both(y_of, at), both(at, y_of), both(z_of, at)
    return np.concatenate([part for table in tables for part in split_np(table)], axis=0)


def lane_roll(value, shift):
    return pltpu.roll(value, shift % 128, value.ndim - 1)


def lane_bit(shape, bit):
    return (lax.broadcasted_iota(jnp.int32, shape, len(shape) - 1) // (1 << bit)) % 2 == 1


def swap_bit(low, high, bit):
    upper = lane_bit(low.shape, bit)
    step = 1 << bit
    return jnp.where(upper, lane_roll(high, step), low), jnp.where(upper, high, lane_roll(low, -step))


def swap_bits(items, pairs):
    items = list(items)
    for index_bit, bit in pairs:
        for at in range(len(items)):
            if not (at >> index_bit) & 1:
                other = at | (1 << index_bit)
                items[at], items[other] = swap_bit(items[at], items[other], bit)
    return items


def halves(value):
    head = value.astype(BF16)
    return head, (value - head.astype(F32)).astype(BF16)


def dot(left, right):
    return lax.dot_general(left, right, (((1,), (0,)), ((), ())), preferred_element_type=F32)


def dot_left(table, value):
    head, rest = (part[...] for part in table)
    value_head, value_rest = halves(value)
    return dot(head, value_head) + (dot(head, value_rest) + dot(rest, value_head))


def dot_right(value, table):
    head, rest = (part[...] for part in table)
    value_head, value_rest = halves(value)
    return dot(value_head, head) + (dot(value_rest, head) + dot(value_head, rest))


def signed(index):
    return jnp.where(index == N // 2, 0, jnp.where(index > N // 2, index - N, index)).astype(F32)


def iota(shape, axis):
    return lax.broadcasted_iota(jnp.int32, shape, axis)


def spread(number):
    return (number & 1) + 2 * (number & 2) + 4 * (number & 4) + 8 * (number & 8)


def gathered_bits(number):
    return (number & 1) + ((number >> 1) & 2) + ((number >> 2) & 4) + ((number >> 3) & 8)


def pack(block, s1, j, first):
    items = swap_bits([block[:, 8 * i : 8 * i + 8] for i in range(4)], [(0, 2), (1, 3)])
    for i in range(4):
        at = 8 * (j % 2 + 2 * i + 8 * (j // 2))
        s1[first : first + block.shape[0], at : at + 8, :] = items[i]


def unpack(r6, cb, j, first, count):
    at = [8 * (j % 2 + 2 * i + 8 * (j // 2)) for i in range(4)]
    items = swap_bits([r6[first : first + count, a : a + 8, :] for a in at], [(0, 2), (1, 3)])
    for i in range(4):
        cb[first : first + count, j, 8 * i : 8 * i + 8, :] = items[i]


def stage_x_pair(r1, s2, table):
    items = [r1[d, pl.ds(e, 64, stride=2), :] for d in range(2) for e in range(2)]
    out = dot_left(table, jnp.concatenate(swap_bits(items, [(0, 2), (1, 3)]), axis=0))
    for q in range(4):
        s2[pl.ds(q, 64, stride=4), :] = out[64 * q : 64 * q + 64]


def stage_x_lone(r1, s2, table):
    items = swap_bits([r1[2, pl.ds(e, 64, stride=2), :] for e in range(2)], [(0, 2)])
    upper = lane_bit((64, 128), 3)
    items = [jnp.where(upper, lane_roll(a, 8), a) for a in items] + [jnp.where(upper, a, lane_roll(a, -8)) for a in items]
    out = dot_left(table, jnp.concatenate(items, axis=0))
    for odd in range(2):
        real, imag = (out[64 * q : 64 * q + 64] for q in (odd, 2 + odd))
        s2[pl.ds(odd, 64, stride=2), :] = jnp.where(upper, imag, real)


def turn(value, bit, sign):
    upper, step = lane_bit(value.shape, bit), 1 << bit
    from_low, from_high = lane_roll(value, step), lane_roll(value, -step)
    return jnp.where(upper, -from_low, from_high) if sign > 0 else jnp.where(upper, from_low, -from_high)


def stage_z_lone(r2, table):
    items = swap_bits([r2[pl.ds(odd, 64, stride=2), :] for odd in range(2)], [(0, 0)])
    upper = lane_bit((64, 128), 1)
    items = [jnp.where(upper, lane_roll(a, 2), a) for a in items] + [jnp.where(upper, a, lane_roll(a, -2)) for a in items]
    value = jnp.concatenate(items, axis=0)
    out = dot_left(table, jnp.concatenate([value, turn(value, 3, 1)], axis=0))
    return jnp.where(lane_bit(out.shape, 1), lane_roll(out, -8), out)


def stage_z_pair(r2, s3, lone, table, zi):
    items = swap_bits([r2[pl.ds(q, 64, stride=4), :] for q in range(4)], [(0, 0), (1, 1)])
    value = jnp.concatenate(items, axis=0)
    out = dot_left(table, jnp.concatenate([value, turn(value, 1, 1)], axis=0))
    wave_x = (2 * zi + iota(out.shape, 1) % 2).astype(F32)
    wave_z = signed(iota(out.shape, 0))
    s3[...] = jnp.where(lane_bit(out.shape, 3), out, wave_x * out + wave_z * lone)


def stage_y(r3, s4, ahead, behind, zi, yi):
    def rows(at):
        return slice(16 * at, 16 * at + 16)

    order = [(0, 0), (1, 1), (2, 3)]
    tiles = [swap_bits([r3[rows(8 * high + low), :] for low in range(8)], order) for high in range(2)]
    left = jnp.concatenate([jnp.concatenate([tiles[0][i], tiles[1][i]], axis=1) for i in range(8)], axis=0)
    out = dot_right(left, ahead).reshape(8, 16, 2 * N)
    by_cos, by_sin = out[..., :N], out[..., N:]
    wave_y = signed(iota((16, N), 1))
    wave_z = signed(16 * yi + iota((16, N), 0))
    fields = [None] * 8
    for odd in range(2):
        wave_x = (2 * zi + odd).astype(F32)
        square_sum = jnp.maximum(wave_x * wave_x + wave_y * wave_y + wave_z * wave_z, 1.0)
        real = [by_cos[4 * c + odd] + by_sin[4 * c + 2 + odd] for c in range(2)]
        imag = [by_cos[4 * c + 2 + odd] - by_sin[4 * c + odd] for c in range(2)]
        for i, part in enumerate((real, imag)):
            potential = (part[0] + wave_y * part[1]) / square_sum
            fields[2 * i + odd] = potential
            fields[4 + 2 * i + odd] = wave_y * potential
    out = dot_right(jnp.concatenate(fields, axis=0), behind).reshape(8, 16, 2 * N)
    by_cos, by_sin = out[..., :N], out[..., N:]
    items = [None] * 8
    for c in range(2):
        for odd in range(2):
            real, imag = 4 * c + odd, 4 * c + 2 + odd
            items[real] = by_cos[real] - by_sin[imag]
            items[imag] = by_cos[imag] + by_sin[real]
    for high in range(2):
        tile = swap_bits([item[:, 128 * high : 128 * high + 128] for item in items], order)
        for low in range(8):
            s4[rows(8 * high + low), :] = tile[low]


def stage_z_back_lone(r4, s5, table):
    value = signed(iota((N, 128), 0)) * r4[...]
    out = dot_left(table, jnp.concatenate([value, turn(value, 1, -1)], axis=0))
    out = [out[64 * i : 64 * i + 64] for i in range(4)]
    high, low = lane_bit((64, 128), 3), lane_bit((64, 128), 1)
    items = []
    for i in range(2):
        real = jnp.where(low, lane_roll(out[2 + i], 2), out[i])
        imag = jnp.where(low, lane_roll(out[2 + i], 8), lane_roll(out[i], 6))
        items.append(jnp.where(high, imag, real))
    items = swap_bits(items, [(0, 0)])
    for odd in range(2):
        s5[pl.ds(odd, 64, stride=2), :] = items[odd]


def stage_z_back_pair(r4, s5, table, zi):
    value = r4[...]
    wave_x = (2 * zi + iota(value.shape, 1) % 2).astype(F32)
    value = jnp.where(lane_bit(value.shape, 3), value, wave_x * value)
    out = dot_left(table, jnp.concatenate([value, turn(value, 1, -1)], axis=0))
    items = swap_bits([out[64 * i : 64 * i + 64] for i in range(4)], [(0, 0), (1, 1)])
    for q in range(4):
        s5[pl.ds(q, 64, stride=4), :] = items[q]


def stage_x_back_lone(r5, s6, table):
    value = jnp.concatenate([r5[pl.ds(odd, 64, stride=2), :] for odd in range(2)], axis=0)
    out = dot_left(table, jnp.concatenate([value, lane_roll(value, -8)], axis=0))
    out = [out[64 * i : 64 * i + 64] for i in range(4)]
    upper = lane_bit((64, 128), 3)
    items = swap_bits([jnp.where(upper, lane_roll(out[2 + i], 8), out[i]) for i in range(2)], [(0, 2)])
    for e in range(2):
        s6[2, pl.ds(e, 64, stride=2), :] = items[e]


def stage_x_back_pair(r5, s6, table):
    value = jnp.concatenate([r5[pl.ds(q, 64, stride=4), :] for q in range(4)], axis=0)
    out = dot_left(table, value)
    items = swap_bits([out[64 * i : 64 * i + 64] for i in range(4)], [(0, 2), (1, 3)])
    for d in range(2):
        for e in range(2):
            s6[d, pl.ds(e, 64, stride=2), :] = items[2 * d + e]


PHASES = 14


def kernel(
    vel_hbm, cnt, tables_hbm, value, kept,
    vel, tables, load, s0, r0, s1, r1, s2p, r2p, s2l, r2l, s3, r3, s4, r4, s5p, r5p, s5l, r5l, s6, r6, cb, r7, send, recv,
):
    loads = [pltpu.make_async_copy(vel_hbm, vel, load.at[0])]
    for table in range(5):
        rows = pl.ds(512 * table, 512)
        loads.append(pltpu.make_async_copy(tables_hbm.at[rows], tables.at[rows], load.at[1 + table]))
    loads[0].start()

    def table(at, columns=slice(0, 512)):
        return tables.at[512 * at : 512 * at + 256, columns], tables.at[512 * at + 256 : 512 * at + 512, columns]

    x_ahead, x_behind = table(0, slice(0, 256)), table(0, slice(256, 512))
    z_ahead, y_ahead, y_behind, z_behind = (table(at) for at in range(1, 5))
    row, col = lax.axis_index("row"), lax.axis_index("col")
    core = row & 1
    px, pz = gathered_bits(row), gathered_bits(row >> 1)
    zi = 8 * pz + (px >> 1)
    yi = 2 * col + core

    def peer_x(step):
        return (row ^ spread(step), col)

    def peer_z(step):
        return (row ^ (4 * spread(step & 7) + 2 * spread(step >> 3)), col)

    def peer_y(step):
        return (row ^ (step & 1), col ^ (step >> 1))

    partner = (row ^ 1, col)

    barrier = pltpu.get_barrier_semaphore()
    for peer, count in ((peer_z, 64), (peer_x, 16), (peer_y, 16)):

        @pl.loop(1, count)
        def _(turn_at, peer=peer, count=count):
            pl.semaphore_signal(barrier, inc=1, device_id=peer(count - turn_at), device_id_type=MESH)

    for item in loads[1:]:
        item.start()
    loads[0].wait()

    def put(source, target, phase, device):
        pltpu.make_async_remote_copy(
            src_ref=source, dst_ref=target, send_sem=send.at[phase], recv_sem=recv.at[phase],
            device_id=device, device_id_type=MESH,
        ).start()

    def keep(source, target, phase):
        pltpu.make_async_copy(source, target, recv.at[phase]).start()

    def arrived(buffer, phase):
        pltpu.make_async_copy(buffer, buffer, recv.at[phase]).wait()

    def left(part, phase):
        pltpu.make_async_copy(part, part, send.at[phase]).wait()

    def spread_out(source, target, phase, me, count, width, peer, part=None):
        def at(ref, place):
            rows = pl.ds(pl.multiple_of(width * place, width), width)
            return ref.at[rows] if part is None else ref.at[part, rows]

        @pl.loop(1, count)
        def _(turn_at):
            step = count - turn_at
            put(at(source, me ^ step), at(target, me), phase, peer(step))

        keep(at(source, me), at(target, me), phase)

    lone, pair = pl.ds(2, 1), pl.ds(0, 2)

    count = cnt[0, 0]
    for i in range(3):
        block = vel[jnp.where(core == 1, jnp.maximum(count - 7 + i, 0), 4 + i)]
        for d in range(3):
            s0[d, i] = block[d]
    pl.semaphore_wait(barrier, 63 + 15 + 15)
    put(s0.at[lone], r0.at[lone], 0, partner)
    put(s0.at[pair], r0.at[pair], 1, partner)

    def bricks(first, number):
        for j in range(4):
            slot = jnp.where(core == 1, count - 4 + j, j)
            owned = jnp.where(core == 1, slot >= 0, j < count)
            mine = vel[jnp.clip(slot, 0, SLOTS - 1)][first : first + number]
            at = jnp.clip(jnp.where(core == 1, j, j - 1), 0, 2)
            theirs = jnp.stack([r0[d, at] for d in range(first, first + number)])
            pack(jnp.where(owned, mine, theirs), s1, j, first)

    arrived(r0.at[lone], 0)
    bricks(2, 1)
    spread_out(s1, r1, 2, px, 16, 8, peer_x, lone)
    arrived(r0.at[pair], 1)
    bricks(0, 2)
    spread_out(s1, r1, 3, px, 16, 8, peer_x, pair)
    for s in range(SLOTS):
        kept[s] = jnp.where(s < count, vel[s], 0.0)

    loads[1].wait()
    arrived(r1.at[lone], 2)
    stage_x_lone(r1, s2l, x_ahead)
    spread_out(s2l, r2l, 4, zi, 64, 2, peer_z)
    arrived(r1.at[pair], 3)
    stage_x_pair(r1, s2p, x_ahead)
    spread_out(s2p, r2p, 5, zi, 64, 4, peer_z)

    loads[2].wait()
    arrived(r2l, 4)
    third = stage_z_lone(r2l, z_ahead)
    arrived(r2p, 5)
    stage_z_pair(r2p, s3, third, z_ahead, zi)
    spread_out(s3, r3, 6, yi, 16, 16, peer_y)

    loads[3].wait()
    loads[4].wait()
    arrived(r3, 6)
    stage_y(r3, s4, y_ahead, y_behind, zi, yi)
    spread_out(s4, r4, 7, yi, 16, 16, peer_y)

    loads[5].wait()
    arrived(r4, 7)
    stage_z_back_lone(r4, s5l, z_behind)
    spread_out(s5l, r5l, 8, zi, 64, 2, peer_z)
    stage_z_back_pair(r4, s5p, z_behind, zi)
    spread_out(s5p, r5p, 9, zi, 64, 4, peer_z)

    arrived(r5l, 8)
    stage_x_back_lone(r5l, s6, x_behind)
    spread_out(s6, r6, 10, px, 16, 8, peer_x, lone)
    arrived(r5p, 9)
    stage_x_back_pair(r5p, s6, x_behind)
    spread_out(s6, r6, 11, px, 16, 8, peer_x, pair)

    theirs = pl.ds(1 - core, 3)
    arrived(r6.at[lone], 10)
    for j in range(4):
        unpack(r6, cb, j, 2, 1)
    put(cb.at[lone, theirs], r7.at[lone], 12, partner)
    arrived(r6.at[pair], 11)
    for j in range(4):
        unpack(r6, cb, j, 0, 2)
    put(cb.at[pair, theirs], r7.at[pair], 13, partner)
    arrived(r7.at[lone], 12)
    arrived(r7.at[pair], 13)
    for s in range(SLOTS):
        key = jnp.where(core == 1, 8 - count, 0) + s
        here, there = jnp.clip(key - 4 * core, 0, 3), jnp.clip(jnp.where(core == 1, key - 1, key - 4), 0, 2)
        for d in range(3):
            block = jnp.where((key >> 2) == core, cb[d, here], r7[d, there])
            value[s, d] = jnp.where(s < count, block, 0.0)

    left(s0.at[lone], 0)
    left(s0.at[pair], 1)
    left(s1.at[lone, pl.ds(0, 120)], 2)
    left(s1.at[pair, pl.ds(0, 120)], 3)
    left(s2l.at[pl.ds(0, 126)], 4)
    left(s2p.at[pl.ds(0, 252)], 5)
    left(s3.at[pl.ds(0, 240)], 6)
    left(s4.at[pl.ds(0, 240)], 7)
    left(s5l.at[pl.ds(0, 126)], 8)
    left(s5p.at[pl.ds(0, 252)], 9)
    left(s6.at[lone, pl.ds(0, 120)], 10)
    left(s6.at[pair, pl.ds(0, 120)], 11)
    left(cb.at[lone, pl.ds(0, 3)], 12)
    left(cb.at[pair, pl.ds(0, 3)], 13)


def body(velocity, counts):
    vmem, hbm = pl.BlockSpec(memory_space=pltpu.VMEM), pl.BlockSpec(memory_space=pltpu.HBM)
    blocks = velocity.reshape(SLOTS, 3, 32, 128)
    shape = jax.ShapeDtypeStruct((SLOTS, 3, 32, 128), F32)
    tables = jnp.asarray(weights())
    part = pltpu.VMEM((3, 3, 32, 128), F32)
    fields = pltpu.VMEM((3, 128, 128), F32)
    full, half = pltpu.VMEM((N, 128), F32), pltpu.VMEM((128, 128), F32)
    value, kept = pl.pallas_call(
        kernel,
        out_shape=(shape, shape),
        in_specs=[hbm, pl.BlockSpec(memory_space=pltpu.SMEM), hbm],
        out_specs=(vmem, vmem),
        scratch_shapes=[
            pltpu.VMEM(shape.shape, F32), pltpu.VMEM(tables.shape, BF16), pltpu.SemaphoreType.DMA((6,)),
            part, part, fields, fields, full, full, half, half, full, full, full, full, full, full, half, half, fields,
            fields, pltpu.VMEM((3, 4, 32, 128), F32), part,
            pltpu.SemaphoreType.DMA((PHASES,)), pltpu.SemaphoreType.DMA((PHASES,)),
        ],
        compiler_params=pltpu.CompilerParams(
            collective_id=0, has_side_effects=True, vmem_limit_bytes=53 * 1024 * 1024
        ),
        name="helmholtz",
    )(blocks, counts, tables)
    comp = value * (1.0 / float(N) ** 3)
    sol = kept - comp
    return comp.reshape(velocity.shape), sol.reshape(velocity.shape)


def solution(mesh):
    blocks, owners = P("col", "row", None, None, None), P("col", "row")
    return jax.shard_map(body, mesh=mesh, in_specs=(blocks, owners), out_specs=(blocks, blocks), check_vma=False)
```

```python
import jax
import jax.numpy as jnp
import ml_dtypes
import numpy as np
from jax import lax
from jax.experimental import pallas as pl
from jax.experimental.pallas import tpu as pltpu
from jax.sharding import PartitionSpec as P

MESH = pl.DeviceIdType.MESH
SLOTS = 7
N = 256
F32 = jnp.float32
BF16 = jnp.bfloat16


def split_np(table):
    head = table.astype(ml_dtypes.bfloat16)
    rest = (table - head.astype(np.float64)).astype(ml_dtypes.bfloat16)
    return head, rest


def weights():
    at = np.arange(N)
    angle = 2 * np.pi * ((at[:, None] * at[None, :]) % N) / N
    cos, sin = np.cos(angle), np.sin(angle)
    high, brick, low = np.meshgrid(np.arange(4), np.arange(16), np.arange(4), indexing="ij")
    x_of = (16 * brick + 4 * high + low).reshape(-1)
    odd, pair = np.meshgrid(np.arange(2), np.arange(64), indexing="ij")
    k_of = (2 * pair + odd).reshape(-1)
    real_rows, imag_rows = cos[:128], -sin[:128].copy()
    imag_rows[0] = cos[128]
    gain = np.full((128, 1), 2.0)
    gain[0] = 1.0
    forward = np.concatenate([real_rows[k_of], imag_rows[k_of]], axis=0)
    back = np.concatenate([(gain * real_rows)[k_of], (gain * imag_rows)[k_of]], axis=0).T
    low, source = np.meshgrid(np.arange(4), np.arange(64), indexing="ij")
    z_of = (4 * source + low).reshape(-1)
    lane = np.arange(N)
    bit = lambda b: (lane >> b) & 1
    y_of = 128 * bit(7) + 64 * bit(3) + 32 * bit(1) + 16 * bit(0) + 8 * bit(2) + ((lane >> 4) & 7)
    both = lambda rows, columns: np.concatenate([t[rows][:, columns] for t in (cos, sin)], axis=1)
    x_both = np.concatenate([forward[:, x_of], back[x_of]], axis=1)
    tables = x_both, both(at, z_of), both(y_of, at), both(at, y_of), both(z_of, at)
    return np.concatenate([part for table in tables for part in split_np(table)], axis=0)


def lane_roll(value, shift):
    return pltpu.roll(value, shift % 128, value.ndim - 1)


def lane_bit(shape, bit):
    return (lax.broadcasted_iota(jnp.int32, shape, len(shape) - 1) & (1 << bit)) != 0


def swap_bit(low, high, bit):
    upper = lane_bit(low.shape, bit)
    step = 1 << bit
    return jnp.where(upper, lane_roll(high, step), low), jnp.where(upper, high, lane_roll(low, -step))


def swap_bits(items, pairs):
    items = list(items)
    for index_bit, bit in pairs:
        for at in range(len(items)):
            if not (at >> index_bit) & 1:
                other = at | (1 << index_bit)
                items[at], items[other] = swap_bit(items[at], items[other], bit)
    return items


def halves(value):
    head = value.astype(BF16)
    return head, (value - head.astype(F32)).astype(BF16)


def dot(left, right):
    return lax.dot_general(left, right, (((1,), (0,)), ((), ())), preferred_element_type=F32)


def dot_left(table, value):
    value_head, value_rest = halves(value)
    first = dot(table[...], value_head)
    return first[:N] + (dot(table[:N, :], value_rest) + first[N:])


def dot_right(value, table):
    rows = value.shape[0]
    value_head, value_rest = halves(value)
    first = dot(jnp.concatenate([value_head, value_rest], axis=0), table[:N, :])
    return first[:rows] + (first[rows:] + dot(value_head, table[N:, :]))


def signed(index):
    return jnp.where(index == N // 2, 0, jnp.where(index > N // 2, index - N, index)).astype(F32)


def iota(shape, axis):
    return lax.broadcasted_iota(jnp.int32, shape, axis)


def spread(number):
    return (number & 1) + 2 * (number & 2) + 4 * (number & 4) + 8 * (number & 8)


def gathered_bits(number):
    return (number & 1) + ((number >> 1) & 2) + ((number >> 2) & 4) + ((number >> 3) & 8)


def pack(block, s1, j, first):
    items = swap_bits([block[:, 8 * i : 8 * i + 8] for i in range(4)], [(0, 2), (1, 3)])
    for i in range(4):
        at = 8 * (j % 2 + 2 * i + 8 * (j // 2))
        s1[first : first + block.shape[0], at : at + 8, :] = items[i]


def unpack(r6, cb, j, first, count):
    at = [8 * (j % 2 + 2 * i + 8 * (j // 2)) for i in range(4)]
    items = swap_bits([r6[first : first + count, a : a + 8, :] for a in at], [(0, 2), (1, 3)])
    for i in range(4):
        cb[first : first + count, j, 8 * i : 8 * i + 8, :] = items[i]


def stage_x_pair(r1, s2, table):
    items = [r1[d, pl.ds(e, 64, stride=2), :] for d in range(2) for e in range(2)]
    out = dot_left(table, jnp.concatenate(swap_bits(items, [(0, 2), (1, 3)]), axis=0))
    for q in range(4):
        s2[pl.ds(q, 64, stride=4), :] = out[64 * q : 64 * q + 64]


def stage_x_lone(r1, s2, table):
    items = swap_bits([r1[2, pl.ds(e, 64, stride=2), :] for e in range(2)], [(0, 2)])
    upper = lane_bit((64, 128), 3)
    items = [jnp.where(upper, lane_roll(a, 8), a) for a in items] + [jnp.where(upper, a, lane_roll(a, -8)) for a in items]
    out = dot_left(table, jnp.concatenate(items, axis=0))
    for odd in range(2):
        real, imag = (out[64 * q : 64 * q + 64] for q in (odd, 2 + odd))
        s2[pl.ds(odd, 64, stride=2), :] = jnp.where(upper, imag, real)


def turn(value, bit, sign):
    upper, step = lane_bit(value.shape, bit), 1 << bit
    from_low, from_high = lane_roll(value, step), lane_roll(value, -step)
    return jnp.where(upper, -from_low, from_high) if sign > 0 else jnp.where(upper, from_low, -from_high)


def stage_z_lone(r2, table):
    items = swap_bits([r2[pl.ds(odd, 64, stride=2), :] for odd in range(2)], [(0, 0)])
    upper = lane_bit((64, 128), 1)
    items = [jnp.where(upper, lane_roll(a, 2), a) for a in items] + [jnp.where(upper, a, lane_roll(a, -2)) for a in items]
    value = jnp.concatenate(items, axis=0)
    out = dot_left(table, jnp.concatenate([value, turn(value, 3, 1)], axis=0))
    return jnp.where(lane_bit(out.shape, 1), lane_roll(out, -8), out)


def stage_z_pair(r2, s3, lone, table, zi):
    items = swap_bits([r2[pl.ds(q, 64, stride=4), :] for q in range(4)], [(0, 0), (1, 1)])
    value = jnp.concatenate(items, axis=0)
    out = dot_left(table, jnp.concatenate([value, turn(value, 1, 1)], axis=0))
    wave_x = (2 * zi + (iota(out.shape, 1) & 1)).astype(F32)
    wave_z = signed(iota(out.shape, 0))
    s3[...] = jnp.where(lane_bit(out.shape, 3), out, wave_x * out + wave_z * lone).reshape(16, 16, 128)


def stage_y(r3, s4, ahead, behind, zi, yi, part):
    rows = slice(8 * part, 8 * part + 8)
    order = [(0, 0), (1, 1), (2, 3)]
    tiles = [swap_bits([r3[8 * high + low, rows, :] for low in range(8)], order) for high in range(2)]
    left = jnp.concatenate([jnp.concatenate([tiles[0][i], tiles[1][i]], axis=1) for i in range(8)], axis=0)
    out = dot_right(left, ahead).reshape(8, 8, 2 * N)
    by_cos, by_sin = out[..., :N], out[..., N:]
    wave_y = signed(iota((8, N), 1))
    wave_z = signed(16 * yi + 8 * part + iota((8, N), 0))
    fields = [None] * 8
    for odd in range(2):
        wave_x = (2 * zi + odd).astype(F32)
        inverse = 1.0 / jnp.maximum(wave_x * wave_x + wave_y * wave_y + wave_z * wave_z, 1.0)
        real = [by_cos[4 * c + odd] + by_sin[4 * c + 2 + odd] for c in range(2)]
        imag = [by_cos[4 * c + 2 + odd] - by_sin[4 * c + odd] for c in range(2)]
        for i, part in enumerate((real, imag)):
            potential = (part[0] + wave_y * part[1]) * inverse
            fields[2 * i + odd] = potential
            fields[4 + 2 * i + odd] = wave_y * potential
    out = dot_right(jnp.concatenate(fields, axis=0), behind).reshape(8, 8, 2 * N)
    by_cos, by_sin = out[..., :N], out[..., N:]
    items = [None] * 8
    for c in range(2):
        for odd in range(2):
            real, imag = 4 * c + odd, 4 * c + 2 + odd
            items[real] = by_cos[real] - by_sin[imag]
            items[imag] = by_cos[imag] + by_sin[real]
    for high in range(2):
        tile = swap_bits([item[:, 128 * high : 128 * high + 128] for item in items], order)
        for low in range(8):
            s4[8 * high + low, rows, :] = tile[low]


def stage_z_back(r4, s5p, s5l, table, zi):
    value = r4[...].reshape(N, 128)
    wave_x = (2 * zi + (iota(value.shape, 1) & 1)).astype(F32)
    third = signed(iota(value.shape, 0)) * value
    value = jnp.where(lane_bit(value.shape, 3), value, wave_x * value)
    both = [jnp.concatenate([part, turn(part, 1, -1)], axis=0) for part in (third, value)]
    both = dot_left(table, jnp.concatenate(both, axis=1))
    out = [both[64 * i : 64 * i + 64, :128] for i in range(4)]
    high, low = lane_bit((64, 128), 3), lane_bit((64, 128), 1)
    items = []
    for i in range(2):
        real = jnp.where(low, lane_roll(out[2 + i], 2), out[i])
        imag = jnp.where(low, lane_roll(out[2 + i], 8), lane_roll(out[i], 6))
        items.append(jnp.where(high, imag, real))
    items = swap_bits(items, [(0, 0)])
    for odd in range(2):
        s5l[pl.ds(odd, 64, stride=2), :] = items[odd]
    items = swap_bits([both[64 * i : 64 * i + 64, 128:] for i in range(4)], [(0, 0), (1, 1)])
    for q in range(4):
        s5p[pl.ds(q, 64, stride=4), :] = items[q]


def stage_x_back_lone(r5, s6, table):
    value = jnp.concatenate([r5[pl.ds(odd, 64, stride=2), :] for odd in range(2)], axis=0)
    out = dot_left(table, jnp.concatenate([value, lane_roll(value, -8)], axis=0))
    out = [out[64 * i : 64 * i + 64] for i in range(4)]
    upper = lane_bit((64, 128), 3)
    items = swap_bits([jnp.where(upper, lane_roll(out[2 + i], 8), out[i]) for i in range(2)], [(0, 2)])
    for e in range(2):
        s6[2, pl.ds(e, 64, stride=2), :] = items[e]


def stage_x_back_pair(r5, s6, table):
    value = jnp.concatenate([r5[pl.ds(q, 64, stride=4), :] for q in range(4)], axis=0)
    out = dot_left(table, value)
    items = swap_bits([out[64 * i : 64 * i + 64] for i in range(4)], [(0, 2), (1, 3)])
    for d in range(2):
        for e in range(2):
            s6[d, pl.ds(e, 64, stride=2), :] = items[2 * d + e]


PHASES = 16


def kernel(
    vel_hbm, cnt, tables_hbm, value, kept,
    vel, tables, load, s0, r0, s1, r1, s2p, r2p, s2l, r2l, s3, r3, s4, r4, s5p, r5p, s5l, r5l, s6, r6, cb, r7, send, recv, ready,
):
    loads = [pltpu.make_async_copy(vel_hbm, vel, load.at[0])]
    for table in range(5):
        rows = pl.ds(512 * table, 512)
        loads.append(pltpu.make_async_copy(tables_hbm.at[rows], tables.at[rows], load.at[1 + table]))
    loads[0].start()

    def table(at, columns=slice(0, 512)):
        return tables.at[512 * at : 512 * at + 512, columns]

    x_ahead, x_behind = table(0, slice(0, 256)), table(0, slice(256, 512))
    z_ahead, y_ahead, y_behind, z_behind = (table(at) for at in range(1, 5))
    row, col = lax.axis_index("row"), lax.axis_index("col")
    core = row & 1
    px, pz = gathered_bits(row), gathered_bits(row >> 1)
    zi = 8 * pz + (px >> 1)
    yi = 2 * col + core

    def peer_x(step):
        return (row ^ spread(step), col)

    def peer_z(step):
        return (row ^ (4 * spread(step & 7) + 2 * spread(step >> 3)), col)

    def peer_brick(step):
        return (row ^ (2 * spread(step)), col)

    def peer_y(step):
        return (row ^ (step & 1), col ^ (step >> 1))

    partner = (row ^ 1, col)

    barrier = pltpu.get_barrier_semaphore()
    for peer, count in ((peer_x, 16), (peer_brick, 8), (peer_y, 16)):

        @pl.loop(1, count)
        def _(turn_at, peer=peer, count=count):
            pl.semaphore_signal(barrier, inc=1, device_id=peer(count - turn_at), device_id_type=MESH)

    for item in loads[1:]:
        item.start()
    loads[0].wait()

    def put(source, target, phase, device):
        pltpu.make_async_remote_copy(
            src_ref=source, dst_ref=target, send_sem=send.at[phase], recv_sem=recv.at[phase],
            device_id=device, device_id_type=MESH,
        ).start()

    def keep(source, target, phase):
        pltpu.make_async_copy(source, target, recv.at[phase]).start()

    def arrived(buffer, phase):
        pltpu.make_async_copy(buffer, buffer, recv.at[phase]).wait()

    def left(part, phase):
        pltpu.make_async_copy(part, part, send.at[phase]).wait()

    def spread_out(source, target, phase, me, count, width, peer, part=None):
        def at(ref, place):
            rows = pl.ds(pl.multiple_of(width * place, width), width)
            return ref.at[rows] if part is None else ref.at[part, rows]

        @pl.loop(1, count)
        def _(turn_at):
            step = count - turn_at
            put(at(source, me ^ step), at(target, me), phase, peer(step))

        keep(at(source, me), at(target, me), phase)

    def spread_y(source, target, phase, part):
        rows = pl.ds(8 * part, 8)

        @pl.loop(1, 16)
        def _(turn_at):
            step = 16 - turn_at
            put(source.at[yi ^ step, rows], target.at[yi, rows], phase, peer_y(step))

        keep(source.at[yi, rows], target.at[yi, rows], phase)

    lone, pair = pl.ds(2, 1), pl.ds(0, 2)

    count = cnt[0, 0]
    for i in range(3):
        block = vel[jnp.where(core == 1, jnp.maximum(count - 7 + i, 0), 4 + i)]
        for d in range(3):
            s0[d, i] = block[d]
    pl.semaphore_wait(barrier, 15 + 7 + 15)
    put(s0.at[lone], r0.at[lone], 0, partner)
    put(s0.at[pair], r0.at[pair], 1, partner)

    @pl.loop(1, 8)
    def _(turn_at):
        pl.semaphore_signal(ready, inc=1, device_id=peer_brick(8 - turn_at), device_id_type=MESH)

    def bricks(first, number):
        for j in range(4):
            slot = jnp.where(core == 1, count - 4 + j, j)
            owned = jnp.where(core == 1, slot >= 0, j < count)
            mine = vel[jnp.clip(slot, 0, SLOTS - 1)][first : first + number]
            at = jnp.clip(jnp.where(core == 1, j, j - 1), 0, 2)
            theirs = jnp.stack([r0[d, at] for d in range(first, first + number)])
            pack(jnp.where(owned, mine, theirs), s1, j, first)

    arrived(r0.at[lone], 0)
    bricks(2, 1)
    spread_out(s1, r1, 2, px, 16, 8, peer_x, lone)
    arrived(r0.at[pair], 1)
    bricks(0, 2)
    spread_out(s1, r1, 3, px, 16, 8, peer_x, pair)
    for s in range(SLOTS):
        kept[s] = jnp.where(s < count, vel[s], 0.0)

    loads[1].wait()
    arrived(r1.at[lone], 2)
    stage_x_lone(r1, s2l, x_ahead)
    pl.semaphore_wait(ready, 7)
    spread_out(s2l, r2l, 4, zi, 64, 2, peer_z)
    arrived(r1.at[pair], 3)
    stage_x_pair(r1, s2p, x_ahead)
    spread_out(s2p, r2p, 5, zi, 64, 4, peer_z)

    loads[2].wait()
    arrived(r2l, 4)
    third = stage_z_lone(r2l, z_ahead)
    arrived(r2p, 5)
    stage_z_pair(r2p, s3, third, z_ahead, zi)
    spread_y(s3, r3, 6, 0)
    spread_y(s3, r3, 14, 1)

    loads[3].wait()
    loads[4].wait()
    for part in range(2):
        arrived(r3.at[:, pl.ds(8 * part, 8)], 6 + 8 * part)
        stage_y(r3, s4, y_ahead, y_behind, zi, yi, part)
        spread_y(s4, r4, 7 + 8 * part, part)

    loads[5].wait()
    arrived(r4.at[:, pl.ds(0, 8)], 7)
    arrived(r4.at[:, pl.ds(8, 8)], 15)
    stage_z_back(r4, s5p, s5l, z_behind, zi)
    spread_out(s5p, r5p, 9, zi, 64, 4, peer_z)
    spread_out(s5l, r5l, 8, zi, 64, 2, peer_z)

    arrived(r5p, 9)
    stage_x_back_pair(r5p, s6, x_behind)
    spread_out(s6, r6, 11, px, 16, 8, peer_x, pair)
    arrived(r5l, 8)
    stage_x_back_lone(r5l, s6, x_behind)
    spread_out(s6, r6, 10, px, 16, 8, peer_x, lone)

    theirs = pl.ds(1 - core, 3)
    arrived(r6.at[pair], 11)
    for j in range(4):
        unpack(r6, cb, j, 0, 2)
    put(cb.at[pair, theirs], r7.at[pair], 13, partner)
    arrived(r6.at[lone], 10)
    for j in range(4):
        unpack(r6, cb, j, 2, 1)
    put(cb.at[lone, theirs], r7.at[lone], 12, partner)
    arrived(r7.at[lone], 12)
    arrived(r7.at[pair], 13)
    for s in range(SLOTS):
        key = jnp.where(core == 1, 8 - count, 0) + s
        here, there = jnp.clip(key - 4 * core, 0, 3), jnp.clip(jnp.where(core == 1, key - 1, key - 4), 0, 2)
        for d in range(3):
            block = jnp.where((key >> 2) == core, cb[d, here], r7[d, there])
            value[s, d] = jnp.where(s < count, block, 0.0)

    left(s0.at[lone], 0)
    left(s0.at[pair], 1)
    left(s1.at[lone, pl.ds(0, 120)], 2)
    left(s1.at[pair, pl.ds(0, 120)], 3)
    left(s2l.at[pl.ds(0, 126)], 4)
    left(s2p.at[pl.ds(0, 252)], 5)
    for part in range(2):
        left(s3.at[pl.ds(0, 15), pl.ds(8 * part, 8)], 6 + 8 * part)
        left(s4.at[pl.ds(0, 15), pl.ds(8 * part, 8)], 7 + 8 * part)
    left(s5l.at[pl.ds(0, 126)], 8)
    left(s5p.at[pl.ds(0, 252)], 9)
    left(s6.at[lone, pl.ds(0, 120)], 10)
    left(s6.at[pair, pl.ds(0, 120)], 11)
    left(cb.at[lone, pl.ds(0, 3)], 12)
    left(cb.at[pair, pl.ds(0, 3)], 13)


def body(velocity, counts):
    vmem, hbm = pl.BlockSpec(memory_space=pltpu.VMEM), pl.BlockSpec(memory_space=pltpu.HBM)
    blocks = velocity.reshape(SLOTS, 3, 32, 128)
    shape = jax.ShapeDtypeStruct((SLOTS, 3, 32, 128), F32)
    tables = jnp.asarray(weights())
    part = pltpu.VMEM((3, 3, 32, 128), F32)
    fields = pltpu.VMEM((3, 128, 128), F32)
    full, half = pltpu.VMEM((N, 128), F32), pltpu.VMEM((128, 128), F32)
    rows_y = pltpu.VMEM((16, 16, 128), F32)
    value, kept = pl.pallas_call(
        kernel,
        out_shape=(shape, shape),
        in_specs=[hbm, pl.BlockSpec(memory_space=pltpu.SMEM), hbm],
        out_specs=(vmem, vmem),
        scratch_shapes=[
            pltpu.VMEM(shape.shape, F32), pltpu.VMEM(tables.shape, BF16), pltpu.SemaphoreType.DMA((6,)),
            part, part, fields, fields, full, full, half, half, rows_y, rows_y, rows_y, rows_y, full, full, half, half,
            fields, fields, pltpu.VMEM((3, 4, 32, 128), F32), part,
            pltpu.SemaphoreType.DMA((PHASES,)), pltpu.SemaphoreType.DMA((PHASES,)), pltpu.SemaphoreType.REGULAR,
        ],
        compiler_params=pltpu.CompilerParams(
            collective_id=0, has_side_effects=True, vmem_limit_bytes=53 * 1024 * 1024
        ),
        name="helmholtz",
    )(blocks, counts, tables)
    comp = value * (1.0 / float(N) ** 3)
    sol = kept - comp
    return comp.reshape(velocity.shape), sol.reshape(velocity.shape)


def solution(mesh):
    blocks, owners = P("col", "row", None, None, None), P("col", "row")
    return jax.shard_map(body, mesh=mesh, in_specs=(blocks, owners), out_specs=(blocks, blocks), check_vma=False)
```
